32 devices in a mesh: groups: 2 (over x), seq: 16 (over z, y, core).
Axes of the slice: x: 2, y: 2, z: 4, core: 2. Of those that a mesh axis runs over, the one named last changes fastest.
Arguments:
- query_raw: bfloat16 [4096, 2048], P(('groups', 'seq')), parts along dimension 0, may hold values from -6 to 6
- key_raw: bfloat16 [4096, 4096], P(('groups', 'seq')), parts along dimension 0, may hold values from -72 to 72
- value_raw: bfloat16 [4096, 4096], P(('groups', 'seq')), parts along dimension 0, may hold values from -6 to 6
- beta_raw: float32 [4096, 32], P(('groups', 'seq')), parts along dimension 0, may hold values from -6 to 1
- gate_raw: float32 [4096, 16], P(('groups', 'seq')), parts along dimension 0, may hold values from 0.3 to 10.6
- conv_weight: float32 [4, 10240], replicated, may hold values from -2.5 to 2.5
- out_grad: bfloat16 [4096, 2048], P(('groups', 'seq')), parts along dimension 0, may hold values from -6 to 6
Outputs:
- mixed: bfloat16 [4096, 2048], P(('groups', 'seq')), parts along dimension 0
- query_grad: bfloat16 [4096, 2048], P(('groups', 'seq')), parts along dimension 0
- key_grad: bfloat16 [4096, 4096], P(('groups', 'seq')), parts along dimension 0
- value_grad: bfloat16 [4096, 4096], P(('groups', 'seq')), parts along dimension 0
- beta_grad: float32 [4096, 32], P(('groups', 'seq')), parts along dimension 0
- gate_grad: float32 [4096, 16], P(('groups', 'seq')), parts along dimension 0
- conv_grad: float32 [8, 10240], P('groups'), parts along dimension 0
The draws below stay inside these ranges and needn't reach their ends.
There are 2 independent parts, one for each index of `groups`. The reference program is written for one: setup_inputs(seed, part) draws one part's arguments, and reference() takes and returns one part's arrays. A program takes and returns all parts, laid end to end along the dimension named above; an argument that names none is the same for every part. Nothing has to cross between parts.
All inputs are finite; a program needn't handle non-finite values.
Results may differ from the reference program's by a relative error of at most 0.001.
Values may be sent and summed in bfloat16 or wider, within the bound.
A program may use at most 384 MiB of HBM per device.

```python
import math
import jax
import jax.numpy as jnp
from jax import lax

SHARD_ATTN_UNITS = 16
DK = 128
DV = 128
KW = 4
TEXT_LENGTH = 2048
CHANNELS = 10240


def head_kinds(key):
    ranks = jax.random.permutation(jax.random.fold_in(key, 11), SHARD_ATTN_UNITS)
    slow_count = jax.random.randint(jax.random.fold_in(key, 5), (), max(1, SHARD_ATTN_UNITS // 4), max(1, 3 * SHARD_ATTN_UNITS // 4) + 1)
    return ranks < slow_count


def draw_gate_raw(key, part):
    slow_heads = head_kinds(key)
    spread = jax.random.uniform(jax.random.fold_in(key, 21), (TEXT_LENGTH, SHARD_ATTN_UNITS), jnp.float32)
    uniform_period = jnp.where(slow_heads[None, :], 9.2 + 1.4 * spread, 2.3 + 1.4 * spread)
    spots = jax.random.randint(jax.random.fold_in(key, 22), (2, SHARD_ATTN_UNITS), 0, TEXT_LENGTH)
    past_only_filter = jnp.any(jnp.arange(TEXT_LENGTH)[:, None, None] == spots[None, :, :], axis=1)
    warmup_period = 0.3 + 1.2 * jax.random.uniform(jax.random.fold_in(key, 23), (TEXT_LENGTH, SHARD_ATTN_UNITS), jnp.float32)
    return jnp.where(past_only_filter, warmup_period, uniform_period).astype(jnp.float32)


def draw_beta_raw(key, part):
    slow_heads = head_kinds(key)
    spread = jax.random.uniform(jax.random.fold_in(key, 41), (TEXT_LENGTH, 2, SHARD_ATTN_UNITS), jnp.float32)
    values = jnp.where(slow_heads[None, None, :], -6.0 + spread, -1.0 + 2.0 * spread)
    return values.reshape(TEXT_LENGTH, 2 * SHARD_ATTN_UNITS).astype(jnp.float32)


def draw_key_raw(key, part):
    noise = jax.random.truncated_normal(jax.random.fold_in(key, 31), -4.0, 4.0, (TEXT_LENGTH, 2 * SHARD_ATTN_UNITS, DK), jnp.float32)
    row_scale = jnp.exp(jax.random.uniform(jax.random.fold_in(key, 32), (TEXT_LENGTH, 2 * SHARD_ATTN_UNITS, 1), jnp.float32, -1.2, 1.2))
    col_scale = jnp.exp(jax.random.uniform(jax.random.fold_in(key, 33), (1, 2 * SHARD_ATTN_UNITS, DK), jnp.float32, -1.2, 1.2))
    values = noise * row_scale * col_scale
    return values.reshape(TEXT_LENGTH, 2 * SHARD_ATTN_UNITS * DK).astype(jnp.bfloat16)


def block_levels(key, dims, cuts, least, top_value):
    factor_of = 1.0
    for dim, blocks in cuts:
        draws = jax.random.uniform(jax.random.fold_in(jax.random.fold_in(key, 6), dim), (blocks,), jnp.float32, least / len(cuts), top_value / len(cuts))
        factor_of = factor_of * jnp.repeat(jnp.exp(draws), dims[dim] // blocks).reshape((-1,) + (1,) * (len(dims) - 1 - dim))
    return factor_of


def gaussian(stream_key, dims, scale, bound, shards=(), dtype=jnp.bfloat16):
    drawn = jax.random.normal(stream_key, dims, jnp.float32) * scale
    if len(shards) > 0:
        drawn = block_levels(stream_key, dims, shards, -0.22, 0.18) * drawn
    return jnp.clip(drawn, min=-bound, max=bound).astype(dtype)


def setup_inputs(seed: int = 0, part: int = 0) -> dict:
    key_of = jax.random.split(jax.random.key(seed), 8)
    own_keys = jax.random.split(jax.random.fold_in(key_of[7], part), 8)
    return {
        "query_raw": gaussian(own_keys[0], (TEXT_LENGTH, SHARD_ATTN_UNITS * DK), 1.0, 6.0, ((0, 16),)),
        "key_raw": draw_key_raw(jax.random.fold_in(jax.random.fold_in(key_of[7], part), 71), part),
        "value_raw": gaussian(own_keys[2], (TEXT_LENGTH, 2 * SHARD_ATTN_UNITS * DV), 1.0, 6.0, ((0, 16),)),
        "beta_raw": draw_beta_raw(jax.random.fold_in(jax.random.fold_in(key_of[7], part), 71), part),
        "gate_raw": draw_gate_raw(jax.random.fold_in(jax.random.fold_in(key_of[7], part), 71), part),
        "conv_weight": gaussian(key_of[5], (KW, CHANNELS), 0.5, 2.5, (), jnp.float32),
        "out_grad": gaussian(own_keys[6], (TEXT_LENGTH, SHARD_ATTN_UNITS * DV), 1.0, 6.0, ((0, 16),)),
    }


highest_precision = lax.Precision.HIGHEST

def token_step(carry_state, block_item):
    queries, key_rows, values, beta_rows, gate_vals = block_item
    key_zero = key_rows[0]
    dot_zero = jnp.einsum('hvk,hk->hv', carry_state, key_zero, precision=highest_precision)
    write_zero = beta_rows[0][:, None] * (values[0] - gate_vals[:, None] * dot_zero)
    carry_state = gate_vals[:, None, None] * carry_state + write_zero[:, :, None] * key_zero[:, None, :]
    key_one = key_rows[1]
    dot_one = jnp.einsum('hvk,hk->hv', carry_state, key_one, precision=highest_precision)
    write_one = beta_rows[1][:, None] * (values[1] - dot_one)
    carry_state = carry_state + write_one[:, :, None] * key_one[:, None, :]
    out_row = jnp.einsum('hvk,hk->hv', carry_state, queries, precision=highest_precision)
    return (carry_state, out_row)

@jax.checkpoint
def run_block(carry_state, block_items):
    return lax.scan(token_step, carry_state, block_items)

def recurrence(queries, key_rows, values, beta_rows, gate_vals):
    span_len = math.gcd(TEXT_LENGTH, 64)
    pieces = TEXT_LENGTH // span_len

    def split_rows(array):
        return array.reshape((pieces, span_len) + array.shape[1:])
    block_items = (split_rows(queries), split_rows(key_rows), split_rows(values), split_rows(beta_rows), split_rows(gate_vals))
    start_state = jnp.zeros((SHARD_ATTN_UNITS, DV, DK), jnp.float32)
    _, out_rows = lax.scan(run_block, start_state, block_items)
    return out_rows.reshape(TEXT_LENGTH, SHARD_ATTN_UNITS * DV)

def forward(query_in, key_in, value_in, beta_in, gate_in, weights):
    joined = jnp.concatenate([query_in, key_in, value_in], axis=1)
    padded = jnp.concatenate([jnp.zeros((KW - 1, joined.shape[1]), jnp.float32), joined], axis=0)
    convolved = weights[0] * padded[0:TEXT_LENGTH]
    for offset in range(1, KW):
        convolved = convolved + weights[offset] * padded[offset:offset + TEXT_LENGTH]
    activated = jax.nn.silu(convolved)
    query_cols = SHARD_ATTN_UNITS * DK
    queries = activated[:, :query_cols].reshape(TEXT_LENGTH, SHARD_ATTN_UNITS, DK)
    key_pre = activated[:, query_cols:3 * query_cols].reshape(TEXT_LENGTH, 2, SHARD_ATTN_UNITS, DK)
    key_rows = key_pre / jnp.sqrt(lax.optimization_barrier(jnp.sum(key_pre * key_pre, axis=-1, keepdims=True)) + 1e-06)
    values = activated[:, 3 * query_cols:].reshape(TEXT_LENGTH, 2, SHARD_ATTN_UNITS, DV)
    beta_rows = jax.nn.sigmoid(beta_in).reshape(TEXT_LENGTH, 2, SHARD_ATTN_UNITS)
    gate_vals = jax.nn.sigmoid(gate_in)
    return recurrence(queries, key_rows, values, beta_rows, gate_vals)

def reference(query_raw, key_raw, value_raw, beta_raw, gate_raw, conv_weight, out_grad):
    mixed_full, back_fn = jax.vjp(forward, query_raw.astype(jnp.float32), key_raw.astype(jnp.float32), value_raw.astype(jnp.float32), beta_raw, gate_raw, conv_weight)
    grads = back_fn(out_grad.astype(jnp.float32))
    return (mixed_full.astype(jnp.bfloat16), grads[0].astype(jnp.bfloat16), grads[1].astype(jnp.bfloat16), grads[2].astype(jnp.bfloat16), grads[3], grads[4], grads[5])
```

```python
import jax
import jax.numpy as jnp
from jax import lax
from jax.sharding import PartitionSpec as P

DK = 128
DV = 128

HIGH = lax.Precision.HIGH
HIGHEST = lax.Precision.HIGHEST


def mm(spec, a, b, precision=HIGH):
    return jnp.einsum(spec, a, b, precision=precision, preferred_element_type=jnp.float32)


def shifted(x, axis, by):
    size = lax.axis_size(axis)
    pairs = [(i, i + by) for i in range(size) if 0 <= i + by < size]
    return lax.ppermute(x, axis, pairs)


def order_of(count):
    index = jnp.arange(count)
    half = count // 2
    return 2 * (index % half) + index // half


def inverse(system):
    count = system.shape[-1]
    place = order_of(count)
    rows, cols = place[:, None], place[None, :]

    def corner(size):
        mask = (rows // (2 * size) == cols // (2 * size)) & (rows // size > cols // size)
        return jnp.where(mask, system, 0.0)

    found = jnp.eye(count, dtype=jnp.float32) - corner(1)
    size = 2
    while size < count:
        found = found - mm("hij,hjk->hik", found, mm("hij,hjk->hik", corner(size), found))
        size *= 2
    return found


@jax.custom_vjp
def solve(system, right):
    return mm("hij,hjk->hik", inverse(system), right)


def solve_fwd(system, right):
    inv = inverse(system)
    out = mm("hij,hjk->hik", inv, right)
    return out, (inv, out)


def solve_bwd(saved, cot):
    inv, out = saved
    right_cot = mm("hji,hjk->hik", inv, cot)
    return -mm("hik,hjk->hij", right_cot, out), right_cot


solve.defvjp(solve_fwd, solve_bwd)


def prepare_feats(extended, weights, beta_in, gate_in):
    tap_count = weights.shape[0]
    tok_rows = extended.shape[0] - tap_count + 1
    convolved = weights[0] * extended[0:tok_rows]
    for offset in range(1, tap_count):
        convolved = convolved + weights[offset] * extended[offset : offset + tok_rows]
    activated = jax.nn.silu(convolved)
    heads = gate_in.shape[1]
    query_cols = heads * DK
    queries = activated[:, :query_cols].reshape(tok_rows, heads, DK).transpose(1, 0, 2)
    key_pre = activated[:, query_cols : 3 * query_cols].reshape(tok_rows, 2, heads, DK)
    key_rows = key_pre / jnp.sqrt(jnp.sum(key_pre * key_pre, axis=-1, keepdims=True) + 1e-06)
    key_rows = key_rows.transpose(2, 1, 0, 3).reshape(heads, 2 * tok_rows, DK)
    values = activated[:, 3 * query_cols :].reshape(tok_rows, 2, heads, DV)
    values = values.transpose(2, 1, 0, 3).reshape(heads, 2 * tok_rows, DV)
    betas = jax.nn.sigmoid(beta_in).reshape(tok_rows, 2, heads)
    betas = betas.transpose(2, 1, 0).reshape(heads, 2 * tok_rows)
    upto = jnp.tril(jnp.ones((tok_rows, tok_rows), jnp.float32))
    cumul = mm("th,st->hs", jax.nn.log_sigmoid(gate_in), upto, HIGHEST)
    return queries, key_rows, values, betas, cumul


def chunk_tables(features):
    queries, keys, values, betas, cumul_tok = features
    count = keys.shape[1]
    place = order_of(count)
    cumul = jnp.concatenate([cumul_tok, cumul_tok], axis=1)
    below = place[:, None] > place[None, :]
    gaps = jnp.where(below, cumul[:, :, None] - cumul[:, None, :], 0.0)
    decay = jnp.where(below, jnp.exp(gaps), 0.0)
    inner = mm("hid,hjd->hij", keys, keys)
    system = jnp.eye(count, dtype=jnp.float32) + betas[:, :, None] * decay * inner
    right = jnp.concatenate(
        [(betas * jnp.exp(cumul))[..., None] * keys, betas[..., None] * values], axis=-1
    )
    solved = solve(system, right)
    w_table, base = solved[..., :DK], solved[..., DK:]
    last = cumul_tok[:, -1:]
    scaled_keys = jnp.exp(last - cumul)[..., None] * keys
    end_gain = jnp.exp(last[:, 0])
    half = count // 2
    reach = place[None, :] <= 2 * jnp.arange(half)[:, None] + 1
    out_logs = jnp.where(reach, cumul_tok[:, :, None] - cumul[:, None, :], 0.0)
    out_mix = jnp.where(reach, jnp.exp(out_logs), 0.0) * mm("hmd,hjd->hmj", queries, keys)
    probe = jnp.exp(cumul_tok)[..., None] * queries
    return probe, out_mix, w_table, base, scaled_keys, end_gain


def run_chunk(state, tables):
    probe, out_mix, w_table, base, scaled_keys, end_gain = tables
    update = base - mm("hcd,hvd->hcv", w_table, state)
    out = mm("hmd,hvd->hmv", probe, state) + mm("hmc,hcv->hmv", out_mix, update)
    final = end_gain[:, None, None] * state + mm("hcv,hcd->hvd", update, scaled_keys)
    return out, final


def chain(mats, offs, grads, axis):
    size = lax.axis_size(axis)
    heads = mats.shape[0]
    parts = max(1, size // heads)
    rows = DV // parts

    def spread(x):
        x = x.reshape((size, heads * parts // size) + x.shape[1:])
        return lax.all_to_all(x, axis, 0, 0)

    def cut(x):
        return x.reshape(heads * parts, rows, DK)

    mats = jnp.repeat(mats, parts, axis=0)
    packed = spread(jnp.concatenate([mats, cut(offs), cut(grads)], axis=1))
    mats, offs, grads = (
        packed[:, :, :DK],
        packed[:, :, DK : DK + rows],
        packed[:, :, DK + rows :],
    )
    states = [jnp.zeros_like(offs[0])]
    for i in range(size - 1):
        states.append(mm("hvk,hkd->hvd", states[-1], mats[i]) + offs[i])
    cots = [jnp.zeros_like(grads[0])]
    for i in range(size - 1, 0, -1):
        cots.append(mm("hvd,hkd->hvk", cots[-1], mats[i]) + grads[i])
    both = jnp.concatenate([jnp.stack(states), jnp.stack(cots[::-1])], axis=2)
    both = lax.all_to_all(both, axis, 0, 0).reshape(heads * parts, 2 * rows, DK)
    return (
        both[:, :rows].reshape(heads, DV, DK),
        both[:, rows:].reshape(heads, DV, DK),
    )


def body(query_raw, key_raw, value_raw, beta_raw, gate_raw, conv_weight, out_grad):
    tok_rows = query_raw.shape[0]
    heads = gate_raw.shape[1]
    margin = conv_weight.shape[0] - 1
    joined = jnp.concatenate([query_raw, key_raw, value_raw], axis=1)
    earlier_rows = shifted(joined[tok_rows - margin :], "seq", 1)
    extended = jnp.concatenate([earlier_rows, joined], axis=0).astype(jnp.float32)
    features, prep_back = jax.vjp(prepare_feats, extended, conv_weight, beta_raw, gate_raw)
    tables, table_back = jax.vjp(chunk_tables, features)
    probe, out_mix, w_table, base, scaled_keys, end_gain = tables
    out_cot = out_grad.astype(jnp.float32).reshape(tok_rows, heads, DV).transpose(1, 0, 2)
    mats = end_gain[:, None, None] * jnp.eye(DK, dtype=jnp.float32) - mm(
        "hck,hcd->hkd", w_table, scaled_keys
    )
    offs = mm("hcv,hcd->hvd", base, scaled_keys)
    mixed_cot = mm("hmv,hmc->hcv", out_cot, out_mix)
    grads = mm("hmv,hmd->hvd", out_cot, probe) - mm("hcv,hcd->hvd", mixed_cot, w_table)
    state_in, carry_grad = chain(mats, offs, grads, "seq")
    (out, _), run_back = jax.vjp(run_chunk, state_in, tables)
    _, table_cots = run_back((out_cot, carry_grad))
    grad_ext, grad_conv, grad_beta, grad_gate = prep_back(table_back(table_cots)[0])
    later_grads = shifted(grad_ext[:margin], "seq", -1)
    grad_joined = grad_ext[margin:].at[tok_rows - margin :].add(later_grads)
    conv_total = lax.psum(grad_conv, "seq")
    mixed = out.transpose(1, 0, 2).reshape(tok_rows, heads * DV)
    query_cols = query_raw.shape[1]
    key_cols = key_raw.shape[1]
    return (
        mixed.astype(jnp.bfloat16),
        grad_joined[:, :query_cols].astype(jnp.bfloat16),
        grad_joined[:, query_cols : query_cols + key_cols].astype(jnp.bfloat16),
        grad_joined[:, query_cols + key_cols :].astype(jnp.bfloat16),
        grad_beta,
        grad_gate,
        conv_total,
    )


def solution(mesh):
    rows = P(("groups", "seq"), None)
    return jax.shard_map(
        body,
        mesh=mesh,
        in_specs=(rows, rows, rows, rows, rows, P(), rows),
        out_specs=(rows, rows, rows, rows, rows, rows, P("groups", None)),
        check_vma=False,
    )
```

```python
import jax
import jax.numpy as jnp
from jax import lax
from jax.sharding import PartitionSpec as P

DK = 128
DV = 128

HIGH = lax.Precision.HIGH
HIGHEST = lax.Precision.HIGHEST


def mm(spec, a, b, precision=HIGH):
    return jnp.einsum(spec, a, b, precision=precision, preferred_element_type=jnp.float32)


def shifted(x, axis, by):
    size = lax.axis_size(axis)
    pairs = [(i, i + by) for i in range(size) if 0 <= i + by < size]
    return lax.ppermute(x, axis, pairs)


def order_of(count):
    index = jnp.arange(count)
    half = count // 2
    return 2 * (index % half) + index // half


def inverse(system):
    count = system.shape[-1]
    place = order_of(count)
    rows, cols = place[:, None], place[None, :]

    def corner(size):
        mask = (rows // (2 * size) == cols // (2 * size)) & (rows // size > cols // size)
        return jnp.where(mask, system, 0.0)

    found = jnp.eye(count, dtype=jnp.float32) - corner(1)
    size = 2
    while size < count:
        found = found - mm("hij,hjk->hik", found, mm("hij,hjk->hik", corner(size), found))
        size *= 2
    return found


@jax.custom_vjp
def solve(system, right):
    return mm("hij,hjk->hik", inverse(system), right)


def solve_fwd(system, right):
    inv = inverse(system)
    out = mm("hij,hjk->hik", inv, right)
    return out, (inv, out)


def solve_bwd(saved, cot):
    inv, out = saved
    right_cot = mm("hji,hjk->hik", inv, cot)
    return -mm("hik,hjk->hij", right_cot, out), right_cot


solve.defvjp(solve_fwd, solve_bwd)


def prepare_feats(extended, weights, beta_in, gate_in):
    tap_count = weights.shape[0]
    tok_rows = extended.shape[0] - tap_count + 1
    convolved = weights[0] * extended[0:tok_rows]
    for offset in range(1, tap_count):
        convolved = convolved + weights[offset] * extended[offset : offset + tok_rows]
    activated = jax.nn.silu(convolved)
    heads = gate_in.shape[1]
    query_cols = heads * DK
    queries = activated[:, :query_cols].reshape(tok_rows, heads, DK).transpose(1, 0, 2)
    key_pre = activated[:, query_cols : 3 * query_cols].reshape(tok_rows, 2, heads, DK)
    key_rows = key_pre / jnp.sqrt(jnp.sum(key_pre * key_pre, axis=-1, keepdims=True) + 1e-06)
    key_rows = key_rows.transpose(2, 1, 0, 3).reshape(heads, 2 * tok_rows, DK)
    values = activated[:, 3 * query_cols :].reshape(tok_rows, 2, heads, DV)
    values = values.transpose(2, 1, 0, 3).reshape(heads, 2 * tok_rows, DV)
    betas = jax.nn.sigmoid(beta_in).reshape(tok_rows, 2, heads)
    betas = betas.transpose(2, 1, 0).reshape(heads, 2 * tok_rows)
    upto = jnp.tril(jnp.ones((tok_rows, tok_rows), jnp.float32))
    cumul = mm("th,st->hs", jax.nn.log_sigmoid(gate_in), upto, HIGHEST)
    return queries, key_rows, values, betas, cumul


def chunk_tables(features):
    queries, keys, values, betas, cumul_tok = features
    count = keys.shape[1]
    place = order_of(count)
    cumul = jnp.concatenate([cumul_tok, cumul_tok], axis=1)
    below = place[:, None] > place[None, :]
    gaps = jnp.where(below, cumul[:, :, None] - cumul[:, None, :], 0.0)
    decay = jnp.where(below, jnp.exp(gaps), 0.0)
    inner = mm("hid,hjd->hij", keys, keys)
    system = jnp.eye(count, dtype=jnp.float32) + betas[:, :, None] * decay * inner
    right = jnp.concatenate(
        [(betas * jnp.exp(cumul))[..., None] * keys, betas[..., None] * values], axis=-1
    )
    solved = solve(system, right)
    w_table, base = solved[..., :DK], solved[..., DK:]
    last = cumul_tok[:, -1:]
    scaled_keys = jnp.exp(last - cumul)[..., None] * keys
    end_gain = jnp.exp(last[:, 0])
    half = count // 2
    reach = place[None, :] <= 2 * jnp.arange(half)[:, None] + 1
    out_logs = jnp.where(reach, cumul_tok[:, :, None] - cumul[:, None, :], 0.0)
    out_mix = jnp.where(reach, jnp.exp(out_logs), 0.0) * mm("hmd,hjd->hmj", queries, keys)
    probe = jnp.exp(cumul_tok)[..., None] * queries
    return probe, out_mix, w_table, base, scaled_keys, end_gain


def run_chunk(state, tables):
    probe, out_mix, w_table, base, scaled_keys, end_gain = tables
    update = base - mm("hcd,hvd->hcv", w_table, state)
    out = mm("hmd,hvd->hmv", probe, state) + mm("hmc,hcv->hmv", out_mix, update)
    final = end_gain[:, None, None] * state + mm("hcv,hcd->hvd", update, scaled_keys)
    return out, final


def chain(mats, offs, grads, axis):
    size = lax.axis_size(axis)
    heads = mats.shape[0]
    parts = max(1, size // heads)
    rows = DV // parts

    def spread(x):
        x = x.reshape((size, heads * parts // size) + x.shape[1:])
        return lax.all_to_all(x, axis, 0, 0)

    def cut(x):
        return x.reshape(heads * parts, rows, DK)

    mats = jnp.repeat(mats, parts, axis=0)
    packed = spread(jnp.concatenate([mats, cut(offs), cut(grads)], axis=1))
    mats, offs, grads = (
        packed[:, :, :DK],
        packed[:, :, DK : DK + rows],
        packed[:, :, DK + rows :],
    )
    states = [jnp.zeros_like(offs[0])]
    for i in range(size - 1):
        states.append(mm("hvk,hkd->hvd", states[-1], mats[i]) + offs[i])
    cots = [jnp.zeros_like(grads[0])]
    for i in range(size - 1, 0, -1):
        cots.append(mm("hvd,hkd->hvk", cots[-1], mats[i]) + grads[i])
    both = jnp.concatenate([jnp.stack(states), jnp.stack(cots[::-1])], axis=2)
    both = lax.all_to_all(both, axis, 0, 0).reshape(heads * parts, 2 * rows, DK)
    return (
        both[:, :rows].reshape(heads, DV, DK),
        both[:, rows:].reshape(heads, DV, DK),
    )


def body(query_raw, key_raw, value_raw, beta_raw, gate_raw, conv_weight, out_grad):
    tok_rows = query_raw.shape[0]
    heads = gate_raw.shape[1]
    margin = conv_weight.shape[0] - 1
    joined = jnp.concatenate([query_raw, key_raw, value_raw], axis=1)
    earlier_rows = shifted(joined[tok_rows - margin :], "seq", 1)
    extended = jnp.concatenate([earlier_rows, joined], axis=0).astype(jnp.float32)
    features, prep_back = jax.vjp(prepare_feats, extended, conv_weight, beta_raw, gate_raw)
    tables, table_back = jax.vjp(chunk_tables, features)
    probe, out_mix, w_table, base, scaled_keys, end_gain = tables
    out_cot = out_grad.astype(jnp.float32).reshape(tok_rows, heads, DV).transpose(1, 0, 2)
    mats = end_gain[:, None, None] * jnp.eye(DK, dtype=jnp.float32) - mm(
        "hck,hcd->hkd", w_table, scaled_keys
    )
    offs = mm("hcv,hcd->hvd", base, scaled_keys)
    mixed_cot = mm("hmv,hmc->hcv", out_cot, out_mix)
    grads = mm("hmv,hmd->hvd", out_cot, probe) - mm("hcv,hcd->hvd", mixed_cot, w_table)
    state_in, carry_grad = chain(mats, offs, grads, "seq")
    (out, _), run_back = jax.vjp(run_chunk, state_in, tables)
    _, table_cots = run_back((out_cot, carry_grad))
    grad_ext, grad_conv, grad_beta, grad_gate = prep_back(table_back(table_cots)[0])
    later_grads = shifted(grad_ext[:margin], "seq", -1)
    grad_joined = grad_ext[margin:] + jnp.pad(later_grads, ((tok_rows - margin, 0), (0, 0)))
    conv_total = lax.psum(grad_conv, "seq")
    mixed = out.transpose(1, 0, 2).reshape(tok_rows, heads * DV)
    query_cols = query_raw.shape[1]
    key_cols = key_raw.shape[1]
    return (
        mixed.astype(jnp.bfloat16),
        grad_joined[:, :query_cols].astype(jnp.bfloat16),
        grad_joined[:, query_cols : query_cols + key_cols].astype(jnp.bfloat16),
        grad_joined[:, query_cols + key_cols :].astype(jnp.bfloat16),
        grad_beta,
        grad_gate,
        conv_total,
    )


def solution(mesh):
    rows = P(("groups", "seq"), None)
    return jax.shard_map(
        body,
        mesh=mesh,
        in_specs=(rows, rows, rows, rows, rows, P(), rows),
        out_specs=(rows, rows, rows, rows, rows, rows, P("groups", None)),
        check_vma=False,
    )
```
